32 devices in a mesh: grp: 2 (over y), aux: 16 (over z, x, core).
Axes of the slice: x: 2, y: 2, z: 4, core: 2. Of those that a mesh axis runs over, the one named last changes fastest.
Arguments:
- three_index: bfloat16 [160, 1024, 1024], P(('grp', 'aux')), parts along dimension 0, may hold values from -6 to 6
- screen: int32 [160, 256], P(('grp', 'aux')), parts along dimension 0, may hold values from 0 to 1, as said below
- orbitals: bfloat16 [2048, 16], P('grp'), parts along dimension 0, may hold values from -1 to 1
- fitting: bfloat16 [160, 80], P(('grp', 'aux')), parts along dimension 0, may hold values from -1 to 1
Outputs:
- exchange_matrix: float32 [2048, 1024], P(('grp', 'aux')), parts along dimension 0
The draws below stay inside these ranges and needn't reach their ends.
There are 2 independent parts, one for each index of `grp`. The reference program is written for one: setup_inputs(seed, part) draws one part's arguments, and reference() takes and returns one part's arrays. A program takes and returns all parts, laid end to end along the dimension named above; each array names one. Nothing has to cross between parts.
Inputs may be any that keep to these rules, and one draw needn't show every extreme that they name: screen[P, a * 16 + a] is 1 for every P and a.
All inputs are finite; a program needn't handle non-finite values.
Results may differ from the reference program's by a relative error of at most 0.0026.
Values may be sent and summed in bfloat16 or wider, within the bound.
A program may use at most 128 MiB of HBM per device.

```python
import jax
import jax.numpy as jnp
from jax import lax

NBF = 1024
BLK = 64
NB = 16
AUX = 80
OCC = 16


def draw_three_index(key, part):
    key = jax.random.fold_in(key, 1)
    first, second, third, fourth = jax.random.split(key, 4)
    places = jnp.arange(NBF).astype(jnp.float32)
    lengths = jnp.exp(jax.random.uniform(first, (AUX, 1, 1), jnp.float32, jnp.log(16.0), jnp.log(NBF / 4.0)))
    gaps = jnp.abs(places[:, None] - places[None, :])
    decay = jnp.exp(-gaps[None, :, :] / lengths) * jnp.sqrt(16.0 / lengths)
    centres = jax.random.uniform(second, (AUX, 1), jnp.float32, 0.0, NBF * 1.0)
    widths = NBF * jnp.exp(jax.random.uniform(third, (AUX, 1), jnp.float32, jnp.log(0.25), 0.0))
    profile = jnp.exp(-jnp.abs(places[None, :] - centres) / widths)
    common = profile[:, :, None] * profile[:, None, :]
    values = jnp.clip(jax.random.normal(fourth, (AUX, NBF, NBF), jnp.float32), -4.0, 4.0)
    strength = 0.15
    return (values * decay + strength * common).astype(jnp.bfloat16)


def draw_screen(key, part):
    key = jax.random.fold_in(key, 2)
    first, second = jax.random.split(key)
    limits = jax.random.randint(first, (AUX, 1), 20, 90)
    rolls = jax.random.randint(second, (AUX, NB * NB), 0, 100)
    places = jnp.arange(NB * NB)
    onside = (places // NB == places % NB)[None, :]
    return jnp.where((rolls < limits) | onside, 1, 0).astype(jnp.int32)


def draw_orbitals(key, part):
    key = jax.random.fold_in(key, 3)
    first, second = jax.random.split(key, 2)
    spacing = NBF / OCC
    jitter = jax.random.uniform(first, (OCC,), jnp.float32, -0.4, 0.4)
    centers = (jnp.arange(OCC).astype(jnp.float32) + 0.5 + jitter) * spacing
    places = jnp.arange(NBF).astype(jnp.float32)
    envelope = jnp.exp(-jnp.abs(places[:, None] - centers[None, :]) / spacing)
    values = jnp.clip(jax.random.normal(second, (NBF, OCC), jnp.float32), -4.0, 4.0)
    return (0.25 * values * envelope).astype(jnp.bfloat16)


def draw_fitting(key, part):
    key = jax.random.fold_in(key, 4)
    first, second = jax.random.split(key)
    places = jnp.arange(AUX)
    onside = (places[:, None] == places[None, :]).astype(jnp.float32)
    gains = jnp.exp(jax.random.uniform(first, (AUX, 1), jnp.float32, jnp.log(0.5), jnp.log(2.0)))
    spread = jnp.clip(jax.random.normal(second, (AUX, AUX), jnp.float32), -4.0, 4.0)
    full = onside * gains + spread * (0.5 / jnp.sqrt(AUX * 1.0))
    return (full / jnp.sqrt(AUX * 1.0)).astype(jnp.bfloat16)


def setup_inputs(seed: int = 0, part: int = 0) -> dict:
    keys = jax.random.split(jax.random.key(seed), 5)
    part_splits = jax.random.split(jax.random.fold_in(keys[4], part), 5)
    return {
        "three_index": draw_three_index(jax.random.fold_in(jax.random.fold_in(keys[4], part), 71), part),
        "screen": draw_screen(jax.random.fold_in(jax.random.fold_in(keys[4], part), 71), part),
        "orbitals": draw_orbitals(jax.random.fold_in(jax.random.fold_in(keys[4], part), 71), part),
        "fitting": draw_fitting(jax.random.fold_in(jax.random.fold_in(keys[4], part), 71), part),
    }


def reference(three_index, screen, orbitals, fitting):
    def one_function(args):
        slab, marks = args
        full_marks = jnp.repeat(jnp.repeat(marks.reshape(NB, NB), BLK, axis=0), BLK, axis=1)
        screened = slab * full_marks.astype(jnp.bfloat16)
        return jnp.dot(screened, orbitals, preferred_element_type=jnp.float32).astype(jnp.bfloat16)

    half_done = lax.map(one_function, (three_index, screen))
    orb_group = 16
    blocks = OCC // orb_group
    stacked = half_done.reshape(AUX, NBF, blocks, orb_group).transpose(2, 0, 1, 3)

    def accumulate(carry, part_block):
        flat_half = part_block.reshape(AUX, NBF * orb_group)
        fitted = jnp.dot(fitting, flat_half, preferred_element_type=jnp.float32).astype(jnp.bfloat16)
        fitted = fitted.reshape(AUX, NBF, orb_group)
        pairs = lax.dot_general(fitted, fitted, (((0, 2), (0, 2)), ((), ())), preferred_element_type=jnp.float32)
        return carry + pairs, None

    initial = jnp.zeros((NBF, NBF), jnp.float32)
    result, unused = lax.scan(accumulate, initial, stacked)
    return result
```

```python
import functools

import jax
import jax.numpy as jnp
from jax import lax
from jax.experimental import pallas as pl
from jax.experimental.pallas import tpu as pltpu
from jax.sharding import PartitionSpec as P

BF = jnp.bfloat16
F32 = jnp.float32
BLK = 64
CHUNK = 256


def iota(shape, dim):
    return lax.broadcasted_iota(jnp.int32, shape, dim)


def kernel(cfg, t_hbm, screen_hbm, orb_hbm, fit_hbm, out_ref, tbuf, screen_v, orb_v, fit_v, wbuf, mbuf, gath,
           fall, kron, ft_s, y_s, t_sem, in_sem, fsend, frecv, send_sem, recv_sem):
    devs, rows, basis, occ, total = cfg
    chunks = basis // CHUNK
    nblk = basis // BLK
    slab = rows * occ
    zs = devs // 4
    me = lax.axis_index("aux")
    z, core = me // 4, me % 2
    xn = me + 2 - 4 * ((me // 2) % 2)
    sib = me + 1 - 2 * core

    small = [
        pltpu.make_async_copy(screen_hbm, screen_v, in_sem.at[0]),
        pltpu.make_async_copy(orb_hbm, orb_v, in_sem.at[1]),
        pltpu.make_async_copy(fit_hbm, fit_v, in_sem.at[2]),
    ]
    for copy in small:
        copy.start()

    def t_copy(k, p):
        part = pl.ds(k * CHUNK, CHUNK)
        return pltpu.make_async_copy(t_hbm.at[p, part], tbuf.at[p, part], t_sem.at[k, p])

    for k in range(chunks):
        for p in range(rows):
            t_copy(k, p).start()

    barrier = pltpu.get_barrier_semaphore()

    @pl.loop(1, devs)
    def _(off):
        pl.semaphore_signal(barrier, inc=1, device_id={"aux": lax.rem(me + off, devs)})

    small[0].wait()
    spread = jnp.where(iota((nblk * nblk, basis), 0) % nblk == iota((nblk * nblk, basis), 1) // BLK, 1.0, 0.0).astype(BF)
    own = iota((16 * nblk, nblk * nblk), 0) // 16 == iota((16 * nblk, nblk * nblk), 1) // nblk
    for p in range(rows):
        marks = jnp.where(own, screen_v[pl.ds(p, 1), :].astype(F32), 0.0).astype(BF)
        mbuf[p] = jnp.dot(marks, spread, preferred_element_type=F32).astype(BF)
    small[1].wait()
    for p in range(rows):
        shift = jnp.where(iota((occ, 128), 0) + occ * p == iota((occ, 128), 1), 1.0, 0.0).astype(BF)
        wbuf[p] = jnp.dot(orb_v[...], shift, preferred_element_type=F32).astype(BF)
    small[2].wait()
    fall[me] = jnp.zeros((16, 128), BF)
    fall[me, pl.ds(0, rows), pl.ds(0, total)] = fit_v[...]

    pl.semaphore_wait(barrier, devs - 1)

    def fit_copy(off):
        return pltpu.make_async_remote_copy(
            src_ref=fall.at[me], dst_ref=fall.at[me], send_sem=fsend.at[off], recv_sem=frecv.at[me],
            device_id={"aux": lax.rem(me + off, devs)})

    @pl.loop(1, devs)
    def _(off):
        fit_copy(off).start()

    def copy(o, k, way, target):
        part = gath.at[k, pl.ds(pl.multiple_of(o * slab, 16), slab), :]
        return pltpu.make_async_remote_copy(
            src_ref=part, dst_ref=part, send_sem=send_sem.at[way, o, k], recv_sem=recv_sem.at[o, k],
            device_id={"aux": target})

    def arrive(o, k):
        copy(o, k, 0, sib).wait_recv()

    def up(o, k, act):
        @pl.when(z < zs - 1)
        def _():
            act(copy(o, k, 0, lax.rem(me + 4, devs)))

    def down(o, k, act):
        @pl.when(z > 0)
        def _():
            act(copy(o, k, 1, lax.rem(me + devs - 4, devs)))

    def across(o, k, act):
        act(copy(o, k, 2, xn))

    def beside(o, k, act):
        act(copy(o, k, 3, sib))

    start = lambda c: c.start()
    finish = lambda c: c.wait_send()

    @pl.loop(0, chunks)
    def _(k):
        total_rows = pl.ds(pl.multiple_of(k * CHUNK, CHUNK), CHUNK)
        acc = jnp.zeros((CHUNK, 128), F32)
        for p in range(rows):
            t_copy(k, p).wait()
            marks = mbuf[p, pl.ds(pl.multiple_of(k * (CHUNK // BLK * 16), 16), CHUNK // BLK * 16), :]
            marks = marks.reshape(CHUNK // BLK, 1, 16, basis)
            lhs = tbuf[p, total_rows, :].reshape(CHUNK // BLK, BLK // 16, 16, basis) * marks
            acc += jnp.dot(lhs.reshape(CHUNK, basis), wbuf[p], preferred_element_type=F32)
        half = jnp.transpose(acc)[:slab].astype(BF)
        gath[k, pl.ds(pl.multiple_of(me * slab, 16), slab), :] = half
        up(me, k, start)
        down(me, k, start)
        across(me, k, start)
        beside(me, k, start)

    def build_kron():
        @pl.loop(1, devs)
        def _(off):
            o = lax.rem(me + off, devs)
            pltpu.make_async_remote_copy(
                src_ref=fall.at[o], dst_ref=fall.at[o], send_sem=fsend.at[off], recv_sem=frecv.at[o],
                device_id={"aux": o}).wait_recv()

        wide = jnp.where(iota((128, devs * slab), 0) == iota((128, devs * slab), 1) // occ, 1.0, 0.0).astype(BF)
        flat = jnp.dot(fall[...].reshape(devs * 16, 128), wide, preferred_element_type=F32).astype(BF)

        @pl.loop(0, devs * slab // 256)
        def _(b):
            q = (iota((256, devs * 16), 0) + b * 256) // occ
            col = iota((256, devs * 16), 1)
            pick = jnp.where((q // rows) * 16 + q % rows == col, 1.0, 0.0).astype(BF)
            full = jnp.dot(pick, flat, preferred_element_type=F32)
            same = iota((256, devs * slab), 0) % occ == iota((256, devs * slab), 1) % occ
            kron[pl.ds(pl.multiple_of(b * 256, 256), 256), :] = jnp.where(same, full, 0.0).astype(BF)

    def each(s, base, act):
        @pl.when(z >= s)
        def _():
            act(lax.rem(base + devs - 4 * s, devs), True)

        if s > 0:
            @pl.when(z + s < zs)
            def _():
                act(lax.rem(base + 4 * s, devs), False)

    for s in range(1, zs + 1):
        @pl.loop(0, chunks)
        def _(k):
            if s < zs:
                def line(o, rising):
                    arrive(o, k)
                    (up if rising else down)(o, k, start)
                    across(o, k, start)
                    beside(o, k, start)
                each(s, me, line)

            def side(o, rising):
                arrive(o, k)
                beside(o, k, start)
            each(s - 1, xn, side)

        if s == 1:
            build_kron()

    @pl.loop(0, devs // 2)
    def _(h):
        for k in range(chunks):
            arrive(2 * h + 1 - core, k)

    per = out_ref.shape[0]
    first = me * per
    lane = pl.multiple_of((first % CHUNK) // 128 * 128, 128)
    mine = gath[first // CHUNK, :, pl.ds(lane, 128)]
    fitted = jnp.dot(kron[...], mine, preferred_element_type=F32)
    ft_s[...] = jnp.transpose(fitted)
    mine_t = ft_s[pl.ds(pl.multiple_of(first % 128, 8), per), :].astype(BF)
    y = jnp.dot(mine_t, kron[...], preferred_element_type=F32)
    high = y.astype(BF)
    y_s[:per] = high
    y_s[per:] = (y - high.astype(F32)).astype(BF)
    for k in range(chunks):
        both = jnp.dot(y_s[...], gath[k], preferred_element_type=F32)
        out_ref[:, k * CHUNK:(k + 1) * CHUNK] = both[:per] + both[per:]

    @pl.loop(0, chunks)
    def _(k):
        up(me, k, finish)
        down(me, k, finish)
        across(me, k, finish)
        beside(me, k, finish)
        for s in range(1, zs + 1):
            if s < zs:
                def line(o, rising):
                    (up if rising else down)(o, k, finish)
                    across(o, k, finish)
                    beside(o, k, finish)
                each(s, me, line)

            def side(o, rising):
                beside(o, k, finish)
            each(s - 1, xn, side)

    @pl.loop(1, devs)
    def _(off):
        fit_copy(off).wait_send()


def gathered(three_index, screen, orbitals, fitting):
    devs = lax.axis_size("aux")
    rows, basis, _ = three_index.shape
    occ = orbitals.shape[1]
    total = fitting.shape[1]
    slab = rows * occ
    chunks = basis // CHUNK
    anywhere = pl.BlockSpec(memory_space=pl.ANY)
    dma = pltpu.SemaphoreType.DMA
    return pl.pallas_call(
        functools.partial(kernel, (devs, rows, basis, occ, total)),
        out_shape=jax.ShapeDtypeStruct((basis // devs, basis), F32),
        in_specs=[anywhere] * 4,
        out_specs=pl.BlockSpec(memory_space=pltpu.VMEM),
        scratch_shapes=[
            pltpu.VMEM(three_index.shape, BF),
            pltpu.VMEM(screen.shape, jnp.int32),
            pltpu.VMEM(orbitals.shape, BF),
            pltpu.VMEM(fitting.shape, BF),
            pltpu.VMEM((rows, basis, 128), BF),
            pltpu.VMEM((rows, 16 * basis // BLK, basis), BF),
            pltpu.VMEM((chunks, devs * slab, CHUNK), BF),
            pltpu.VMEM((devs, 16, 128), BF),
            pltpu.VMEM((devs * slab, devs * slab), BF),
            pltpu.VMEM((128, devs * slab), F32),
            pltpu.VMEM((2 * basis // devs, devs * slab), BF),
            dma((chunks, rows)),
            dma((3,)),
            dma((devs,)),
            dma((devs,)),
            dma((4, devs, chunks)),
            dma((devs, chunks)),
        ],
        compiler_params=pltpu.CompilerParams(
            collective_id=0, has_side_effects=True, vmem_limit_bytes=48 * 1024 * 1024),
        cost_estimate=pl.CostEstimate(
            flops=2 * rows * basis * basis * occ, bytes_accessed=2 * rows * basis * basis, transcendentals=0),
    )(three_index, screen, orbitals, fitting)


def by_orbital(three_index, screen, orbitals, fitting):
    aux_count = lax.axis_size("aux")
    aux_rows, basis_count, _ = three_index.shape
    block_count = basis_count // BLK
    orb_dev = orbitals.shape[1] // aux_count
    total_aux = fitting.shape[1]
    screen_full = screen.reshape(aux_rows, block_count, 1, block_count, 1).astype(BF)
    screen_full = jnp.broadcast_to(screen_full, (aux_rows, block_count, BLK, block_count, BLK))
    screened = three_index * screen_full.reshape(aux_rows, basis_count, basis_count)
    half = jnp.einsum("pmn,ni->pmi", screened, orbitals, preferred_element_type=F32).astype(BF)
    half = half.reshape(aux_rows, basis_count, aux_count, orb_dev)
    half = lax.all_to_all(half, "aux", split_axis=2, concat_axis=0, tiled=True)
    flat = half.reshape(total_aux, basis_count * orb_dev)
    whole_fit = lax.all_gather(fitting, "aux", axis=0, tiled=True)
    fitted = jnp.dot(whole_fit, flat, preferred_element_type=F32).astype(BF)
    fitted = fitted.reshape(whole_fit.shape[0], basis_count, orb_dev)
    partial_value = lax.dot_general(fitted, fitted, (((0, 2), (0, 2)), ((), ())), preferred_element_type=F32)
    return lax.psum_scatter(partial_value, "aux", scatter_dimension=0, tiled=True)


def shards(three_index, screen, orbitals, fitting):
    devs = lax.axis_size("aux")
    rows, basis, _ = three_index.shape
    slab = rows * orbitals.shape[1]
    fits = (
        devs % 4 == 0 and slab <= 128 and slab % 16 == 0 and rows <= 16 and fitting.shape[1] <= 128
        and basis % CHUNK == 0 and (devs * slab) % 256 == 0 and 128 % (basis // devs) == 0
        and rows * basis * basis + (basis + devs * slab) * devs * slab <= 12 * 1024 * 1024
    )
    return (gathered if fits else by_orbital)(three_index, screen, orbitals, fitting)


def solution(mesh):
    return jax.shard_map(
        shards,
        mesh=mesh,
        in_specs=(
            P(("grp", "aux"), None, None),
            P(("grp", "aux"), None),
            P("grp", None),
            P(("grp", "aux"), None),
        ),
        out_specs=P(("grp", "aux"), None),
        check_vma=False,
    )
```

```python
import functools

import jax
import jax.numpy as jnp
from jax import lax
from jax.experimental import pallas as pl
from jax.experimental.pallas import tpu as pltpu
from jax.sharding import PartitionSpec as P

BF = jnp.bfloat16
F32 = jnp.float32
BLK = 64
CHUNK = 512
CROSS = 0
REV = False


def iota(shape, dim):
    return lax.broadcasted_iota(jnp.int32, shape, dim)


def kernel(cfg, t_hbm, screen_hbm, orb_hbm, fit_hbm, out_ref, tbuf, screen_v, orb_v, fit_v, wbuf, mbuf, gath,
           fall, fit_s, mine_s, ft_s, y_s, t_sem, in_sem, fsend, frecv, send_sem, recv_sem):
    devs, rows, basis, occ, total = cfg
    chunks = basis // CHUNK
    nblk = basis // BLK
    slab = rows * occ
    zs = devs // 4
    me = lax.axis_index("aux")
    z, core = me // 4, me % 2
    xn = me + 2 - 4 * ((me // 2) % 2)
    sib = me + 1 - 2 * core

    small = [
        pltpu.make_async_copy(screen_hbm, screen_v, in_sem.at[0]),
        pltpu.make_async_copy(orb_hbm, orb_v, in_sem.at[1]),
        pltpu.make_async_copy(fit_hbm, fit_v, in_sem.at[2]),
    ]
    for copy in small:
        copy.start()

    def t_copy(k, p):
        part = pl.ds(k * CHUNK, CHUNK)
        return pltpu.make_async_copy(t_hbm.at[p, part], tbuf.at[p, part], t_sem.at[k, p])

    for k in range(chunks):
        for p in range(rows):
            t_copy(k, p).start()

    barrier = pltpu.get_barrier_semaphore()

    @pl.loop(1, devs)
    def _(off):
        pl.semaphore_signal(barrier, inc=1, device_id={"aux": lax.rem(me + off, devs)})

    small[0].wait()
    spread = jnp.where(iota((nblk * nblk, basis), 0) % nblk == iota((nblk * nblk, basis), 1) // BLK, 1.0, 0.0).astype(BF)
    own = iota((16 * nblk, nblk * nblk), 0) // 16 == iota((16 * nblk, nblk * nblk), 1) // nblk
    for p in range(rows):
        marks = jnp.where(own, screen_v[pl.ds(p, 1), :].astype(F32), 0.0).astype(BF)
        mbuf[p] = jnp.dot(marks, spread, preferred_element_type=F32).astype(BF)
    small[1].wait()
    for p in range(rows):
        shift = jnp.where(iota((occ, 128), 0) + occ * p == iota((occ, 128), 1), 1.0, 0.0).astype(BF)
        wbuf[p] = lax.dot_general(
            orb_v[...], shift, (((0,), (0,)), ((), ())), preferred_element_type=F32).astype(BF)
    small[2].wait()
    fall[me] = jnp.zeros((16, 128), BF)
    fall[me, pl.ds(0, rows), pl.ds(0, total)] = fit_v[...]

    pl.semaphore_wait(barrier, devs - 1)

    def fit_copy(off):
        return pltpu.make_async_remote_copy(
            src_ref=fall.at[me], dst_ref=fall.at[me], send_sem=fsend.at[off], recv_sem=frecv.at[me],
            device_id={"aux": lax.rem(me + off, devs)})

    @pl.loop(1, devs)
    def _(off):
        fit_copy(off).start()

    def copy(o, k, way, target):
        part = gath.at[k, pl.ds(pl.multiple_of(o * slab, 16), slab), :]
        return pltpu.make_async_remote_copy(
            src_ref=part, dst_ref=part, send_sem=send_sem.at[way, o, k], recv_sem=recv_sem.at[o, k],
            device_id={"aux": target})

    def arrive(o, k):
        copy(o, k, 0, sib).wait_recv()

    def up(o, k, act):
        @pl.when(z < zs - 1)
        def _():
            act(copy(o, k, 0, lax.rem(me + 4, devs)))

    def down(o, k, act):
        @pl.when(z > 0)
        def _():
            act(copy(o, k, 1, lax.rem(me + devs - 4, devs)))

    def across(o, k, act):
        act(copy(o, k, 2, xn))

    def beside(o, k, act):
        act(copy(o, k, 3, sib))

    start = lambda c: c.start()
    finish = lambda c: c.wait_send()

    @pl.loop(0, chunks)
    def _(k):
        total_rows = pl.ds(pl.multiple_of(k * CHUNK, CHUNK), CHUNK)
        acc = jnp.zeros((CHUNK, 128), F32)
        for p in range(rows):
            t_copy(k, p).wait()
            marks = mbuf[p, pl.ds(pl.multiple_of(k * (CHUNK // BLK * 16), 16), CHUNK // BLK * 16), :]
            marks = marks.reshape(CHUNK // BLK, 1, 16, basis)
            lhs = tbuf[p, total_rows, :].reshape(CHUNK // BLK, BLK // 16, 16, basis) * marks
            acc += jnp.dot(lhs.reshape(CHUNK, basis), wbuf[p], preferred_element_type=F32)
        half = jnp.transpose(acc)[:slab].astype(BF)
        gath[k, pl.ds(pl.multiple_of(me * slab, 16), slab), :] = half
        up(me, k, start)
        down(me, k, start)
        across(me, k, start)
        beside(me, k, start)

    def build_fit():
        @pl.loop(1, devs)
        def _(off):
            o = lax.rem(me + off, devs)
            pltpu.make_async_remote_copy(
                src_ref=fall.at[o], dst_ref=fall.at[o], send_sem=fsend.at[off], recv_sem=frecv.at[o],
                device_id={"aux": o}).wait_recv()

        q, col = iota((total, devs * 16), 0), iota((total, devs * 16), 1)
        pick = jnp.where((q // rows) * 16 + q % rows == col, 1.0, 0.0).astype(BF)
        fit_s[...] = jnp.dot(pick, fall[...].reshape(devs * 16, 128), preferred_element_type=F32).astype(BF)

    def each(s, base, act):
        @pl.when(z >= s)
        def _():
            act(lax.rem(base + devs - 4 * s, devs), True)

        if s > 0:
            @pl.when(z + s < zs)
            def _():
                act(lax.rem(base + 4 * s, devs), False)

    def relay(s, k, act, waits):
        late = k >= chunks - CROSS

        def line(o, rising):
            waits(o, k)
            (up if rising else down)(o, k, act)
            if not late:
                across(o, k, act)
            beside(o, k, act)

        def side(o, rising):
            waits(o, k)
            if late and s == 1:
                up(o, k, act)
                down(o, k, act)
            elif late:
                (up if rising else down)(o, k, act)
            beside(o, k, act)

        if late:
            each(s - 1, xn, side)
        if s < zs:
            each(s, me, line)
        if not late:
            each(s - 1, xn, side)

    for s in range(1, zs + 1):
        for k in reversed(range(chunks)) if s == 1 and REV else range(chunks):
            relay(s, k, start, arrive)
        if s == 1:
            build_fit()

    @pl.loop(0, devs // 2)
    def _(h):
        for k in range(chunks):
            arrive(2 * h + 1 - core, k)

    per = out_ref.shape[0]
    first = me * per
    lane = pl.multiple_of((first % CHUNK) // 128 * 128, 128)
    mine_s[...] = gath[first // CHUNK, :, pl.ds(lane, 128)].astype(F32)
    mine = jnp.concatenate([mine_s[pl.ds(i, total, occ), :].astype(BF) for i in range(occ)], axis=1)
    fitted = jnp.dot(fit_s[:, :total], mine, preferred_element_type=F32).astype(BF)
    back = lax.dot_general(fit_s[...], fitted, (((0,), (0,)), ((), ())), preferred_element_type=F32)
    for i in range(occ):
        mine_s[pl.ds(i, total, occ), :] = back[:total, i * 128:(i + 1) * 128]
    ft_s[...] = jnp.transpose(mine_s[...])
    y = ft_s[pl.ds(pl.multiple_of(first % 128, 8), per), :]
    high = y.astype(BF)
    y_s[:per] = high
    y_s[per:] = (y - high.astype(F32)).astype(BF)
    for k in range(chunks):
        both = jnp.dot(y_s[...], gath[k], preferred_element_type=F32)
        out_ref[:, k * CHUNK:(k + 1) * CHUNK] = both[:per] + both[per:]

    for k in range(chunks):
        up(me, k, finish)
        down(me, k, finish)
        across(me, k, finish)
        beside(me, k, finish)
        for s in range(1, zs + 1):
            relay(s, k, finish, lambda o, k: None)

    @pl.loop(1, devs)
    def _(off):
        fit_copy(off).wait_send()


def gathered(three_index, screen, orbitals, fitting):
    devs = lax.axis_size("aux")
    rows, basis, _ = three_index.shape
    occ = orbitals.shape[1]
    total = fitting.shape[1]
    slab = rows * occ
    chunks = basis // CHUNK
    anywhere = pl.BlockSpec(memory_space=pltpu.HBM)
    dma = pltpu.SemaphoreType.DMA
    return pl.pallas_call(
        functools.partial(kernel, (devs, rows, basis, occ, total)),
        out_shape=jax.ShapeDtypeStruct((basis // devs, basis), F32),
        in_specs=[anywhere] * 4,
        out_specs=pl.BlockSpec(memory_space=pltpu.VMEM),
        scratch_shapes=[
            pltpu.VMEM(three_index.shape, BF),
            pltpu.VMEM(screen.shape, jnp.int32),
            pltpu.VMEM((occ, basis), BF),
            pltpu.VMEM(fitting.shape, BF),
            pltpu.VMEM((rows, basis, 128), BF),
            pltpu.VMEM((rows, 16 * basis // BLK, basis), BF),
            pltpu.VMEM((chunks, devs * slab, CHUNK), BF),
            pltpu.VMEM((devs, 16, 128), BF),
            pltpu.VMEM((total, 128), BF),
            pltpu.VMEM((devs * slab, 128), F32),
            pltpu.VMEM((128, devs * slab), F32),
            pltpu.VMEM((2 * basis // devs, devs * slab), BF),
            dma((chunks, rows)),
            dma((3,)),
            dma((devs,)),
            dma((devs,)),
            dma((4, devs, chunks)),
            dma((devs, chunks)),
        ],
        compiler_params=pltpu.CompilerParams(
            collective_id=0, has_side_effects=True, vmem_limit_bytes=62 * 1024 * 1024),
        cost_estimate=pl.CostEstimate(
            flops=2 * rows * basis * basis * occ, bytes_accessed=2 * rows * basis * basis, transcendentals=0),
    )(three_index, screen, orbitals.T, fitting)


def by_orbital(three_index, screen, orbitals, fitting):
    aux_count = lax.axis_size("aux")
    aux_rows, basis_count, _ = three_index.shape
    block_count = basis_count // BLK
    orb_dev = orbitals.shape[1] // aux_count
    total_aux = fitting.shape[1]
    screen_full = screen.reshape(aux_rows, block_count, 1, block_count, 1).astype(BF)
    screen_full = jnp.broadcast_to(screen_full, (aux_rows, block_count, BLK, block_count, BLK))
    screened = three_index * screen_full.reshape(aux_rows, basis_count, basis_count)
    half = jnp.einsum("pmn,ni->pmi", screened, orbitals, preferred_element_type=F32).astype(BF)
    half = half.reshape(aux_rows, basis_count, aux_count, orb_dev)
    half = lax.all_to_all(half, "aux", split_axis=2, concat_axis=0, tiled=True)
    flat = half.reshape(total_aux, basis_count * orb_dev)
    whole_fit = lax.all_gather(fitting, "aux", axis=0, tiled=True)
    fitted = jnp.dot(whole_fit, flat, preferred_element_type=F32).astype(BF)
    fitted = fitted.reshape(whole_fit.shape[0], basis_count, orb_dev)
    partial_value = lax.dot_general(fitted, fitted, (((0, 2), (0, 2)), ((), ())), preferred_element_type=F32)
    return lax.psum_scatter(partial_value, "aux", scatter_dimension=0, tiled=True)


def shards(three_index, screen, orbitals, fitting):
    devs = lax.axis_size("aux")
    rows, basis, _ = three_index.shape
    slab = rows * orbitals.shape[1]
    fits = (
        devs % 4 == 0 and slab <= 128 and slab % 16 == 0 and rows <= 16 and fitting.shape[1] <= 128 and fitting.shape[1] == devs * rows
        and basis % CHUNK == 0 and (devs * slab) % 256 == 0 and 128 % (basis // devs) == 0
        and rows * basis * basis + basis * devs * slab <= 12 * 1024 * 1024
    )
    return (gathered if fits else by_orbital)(three_index, screen, orbitals, fitting)


def solution(mesh):
    return jax.shard_map(
        shards,
        mesh=mesh,
        in_specs=(
            P(("grp", "aux"), None, None),
            P(("grp", "aux"), None),
            P("grp", None),
            P(("grp", "aux"), None),
        ),
        out_specs=P(("grp", "aux"), None),
        check_vma=False,
    )
```
